32 devices in a mesh: groups: 2 (over y), sector: 4 (over z), block: 2 (over x), rep: 2 (over core).
Axes of the slice: x: 2, y: 2, z: 4, core: 2. Of those that a mesh axis runs over, the one named last changes fastest.
Arguments:
- corner: bfloat16 [8, 512, 4096], P(('groups', 'sector'), 'block', 'rep'), parts along dimension 0, may hold values from -6 to 6
- site: bfloat16 [16, 512, 128], P('groups'), parts along dimension 0, may hold values from -0.03125 to 0.03125
- projector: bfloat16 [8, 128, 128], P(('groups', 'sector')), parts along dimension 0, may hold values from -0.5 to 0.5
- cotangent: bfloat16 [8, 512, 128], P(('groups', 'sector'), 'block'), parts along dimension 0, may hold values from -6 to 6
- sector_dim: int32 [8], P(('groups', 'sector')), parts along dimension 0, may hold values from 32 to 128, as said below
- pair_dest: int32 [1024], P(('groups', 'sector', 'rep')), parts along dimension 0, may hold values from 0 to 3
- pair_sub: int32 [1024], P(('groups', 'sector', 'rep')), parts along dimension 0, may hold values from 0 to 3
- pair_site: int32 [1024], P(('groups', 'sector', 'rep')), parts along dimension 0, may hold values from 0 to 7
Outputs:
- corner_new: bfloat16 [8, 512, 128], P(('groups', 'sector'), 'block'), parts along dimension 0
- corner_grad: bfloat16 [8, 512, 4096], P(('groups', 'sector'), 'block', 'rep'), parts along dimension 0
- site_grad: float32 [16, 512, 128], P('groups', 'sector'), parts along dimension 0
The draws below stay inside these ranges and needn't reach their ends.
There are 2 independent parts, one for each index of `groups`. The reference program is written for one: setup_inputs(seed, part) draws one part's arguments, and reference() takes and returns one part's arrays. A program takes and returns all parts, laid end to end along the dimension named above; each array names one. Nothing has to cross between parts.
Inputs may be any that keep to these rules, and one draw needn't show every extreme that they name: `sector_dim`: one sector in every draw keeps all 128 states.
All inputs are finite; a program needn't handle non-finite values.
Results may differ from the reference program's by a relative error of at most 0.008.
Values may be sent and summed in bfloat16 or wider, within the bound.
No kernel may reach another device: no remote copies, remote signals or barrier semaphores. Data moves between devices by JAX's collectives and lax.ppermute only.
A program may use at most 64 MiB of HBM per device.

```python
import math
import jax
import jax.numpy as jnp
import numpy as np
from jax import lax

CHIS = 128
KSUB = 512
NK = 8
NG = 8
PAIR_DEV = 64
NKR = 4
KIN = 4096
ROWS = 512
NSEC = 4
NPAIR = 512
N_REP = 2


def draw_sector_dim(key, part):
    key = jax.random.fold_in(key, 11)
    first, second = jax.random.split(key)
    values = jax.random.randint(first, (NSEC,), CHIS // 4, CHIS + 1)
    chosen = jax.random.randint(second, (), 0, NSEC)
    return jnp.where(jnp.arange(NSEC) == chosen, CHIS, values).astype(jnp.int32)


def with_ends(array, stream_key, smallest, largest):
    dims = array.shape
    index_at = [jax.random.randint(jax.random.fold_in(stream_key, axis), (), 0, dims[axis]) for axis in range(len(dims))]
    array = array.at[tuple(index_at)].set(smallest)
    longest = dims.index(max(dims))
    index_at[longest] = (index_at[longest] + 1) % dims[longest]
    return array.at[tuple(index_at)].set(largest)


def levels(own_key, extent, shards, least, high):
    def one(axis_at, blocks):
        heights = jax.random.uniform(jax.random.fold_in(jax.random.fold_in(own_key, 6), axis_at), (blocks,), jnp.float32, least / len(shards), high / len(shards))
        return jnp.repeat(jnp.exp(heights), extent[axis_at] // blocks).reshape((-1,) + (1,) * (len(extent) - axis_at - 1))

    loudness = one(*shards[0])
    for cut in shards[1:]:
        loudness = loudness * one(*cut)
    return loudness


def rank_table(amount, lean):
    weights = [(1 << 20) // math.isqrt(standing ** lean) + 1 for standing in range(1, amount + 1)]
    scale = 1 + sum(weights) // (1 << 30)
    return np.cumsum(np.array([max(1, weight // scale) for weight in weights]))


def skewed_ids(rng, dims, amount, lean):
    grid = rank_table(amount, lean)
    ticket = jax.random.randint(jax.random.fold_in(rng, 1), dims, 0, int(grid[amount - 1]))
    rank = jnp.searchsorted(jnp.asarray(grid, jnp.int32), ticket, side="right")
    return jax.random.permutation(jax.random.fold_in(rng, 2), amount)[rank].astype(jnp.int32)


def bell_draw(rng, shape, width, limit, pieces=(), kind=jnp.bfloat16):
    gain = levels(rng, shape, pieces, -0.22, 0.18) if pieces else 1.0
    values = jax.random.normal(rng, shape, jnp.float32) * width * gain
    return jnp.minimum(jnp.maximum(values, -limit), limit).astype(kind)


def setup_inputs(seed: int = 0, part: int = 0) -> dict:
    splits = jax.random.split(jax.random.key(seed), 9)
    part_keys = jax.random.split(jax.random.fold_in(splits[8], part), 9)
    return {
        "corner": bell_draw(part_keys[0], (NSEC, ROWS, KIN), 1.0, 6.0, ((0, 4), (1, 2), (2, 2))),
        "site": bell_draw(part_keys[1], (NG, KSUB, CHIS), (KSUB * PAIR_DEV) ** -0.5, 0.03125),
        "projector": bell_draw(part_keys[2], (NSEC, CHIS, CHIS), CHIS ** -0.5, 0.5, ((0, 4),)),
        "cotangent": bell_draw(part_keys[3], (NSEC, ROWS, CHIS), 1.0, 6.0, ((0, 4), (1, 2))),
        "sector_dim": draw_sector_dim(jax.random.fold_in(jax.random.fold_in(splits[8], part), 71), part),
        "pair_dest": with_ends(skewed_ids(part_keys[5], (NPAIR,), NSEC, 2), jax.random.fold_in(part_keys[5], 3), 0, NSEC - 1).astype(jnp.int32),
        "pair_sub": with_ends(jax.random.randint(part_keys[6], (NPAIR,), 0, NKR), jax.random.fold_in(part_keys[6], 1), 0, NKR - 1).astype(jnp.int32),
        "pair_site": with_ends(jax.random.randint(part_keys[7], (NPAIR,), 0, NG), jax.random.fold_in(part_keys[7], 1), 0, NG - 1).astype(jnp.int32),
    }


def reference(corner, site, projector, cotangent, sector_dim, pair_dest, pair_sub, pair_site):
    highest = lax.Precision.HIGHEST
    per_source = PAIR_DEV * N_REP
    position = jnp.arange(NPAIR, dtype=jnp.int32)
    sub_global = NKR * ((position // PAIR_DEV) % N_REP) + pair_sub
    combo_index = sub_global * NG + pair_site
    dest_hot = (pair_dest[:, None] == jnp.arange(NSEC, dtype=jnp.int32)[None, :]).astype(jnp.float32)
    combo_hot = (combo_index[:, None] == jnp.arange(NK * NG, dtype=jnp.int32)[None, :]).astype(jnp.float32)
    counts = jnp.einsum("apb,apq->abq", dest_hot.reshape(NSEC, per_source, NSEC),
                        combo_hot.reshape(NSEC, per_source, NK * NG), precision=highest)
    live_cols = (jnp.arange(CHIS, dtype=jnp.int32)[None, :] < sector_dim[:, None]).astype(jnp.bfloat16)
    site_wide = site.astype(jnp.float32)

    def forward(source):
        slices = corner[source].astype(jnp.float32).reshape(ROWS, NK, KSUB)
        products = jnp.einsum("rki,gic->kgrc", slices, site_wide, precision=highest).reshape(NK * NG, ROWS, CHIS)
        return jnp.einsum("bq,qrc->brc", counts[source], products, precision=highest).astype(jnp.bfloat16)

    partials = lax.map(forward, jnp.arange(NSEC, dtype=jnp.int32))
    enlarged = jnp.sum(partials.astype(jnp.float32), axis=0).astype(jnp.bfloat16)
    projected = jnp.einsum("brc,bcd->brd", enlarged.astype(jnp.float32), projector.astype(jnp.float32), precision=highest)
    corner_new = (projected * live_cols[:, None, :].astype(jnp.float32)).astype(jnp.bfloat16)
    masked = (cotangent * live_cols[:, None, :]).astype(jnp.float32)
    grad_enlarged = jnp.einsum("brc,bdc->brd", masked, projector.astype(jnp.float32), precision=highest).astype(jnp.bfloat16)
    grad_wide = grad_enlarged.astype(jnp.float32)

    def backward(carry, source):
        pulled = jnp.einsum("bq,brc->qrc", counts[source], grad_wide, precision=highest).astype(jnp.bfloat16)
        pulled_wide = pulled.astype(jnp.float32).reshape(NK, NG, ROWS, CHIS)
        grad_cols = jnp.einsum("kgrc,gic->rki", pulled_wide, site_wide, precision=highest)
        slices = corner[source].astype(jnp.float32).reshape(ROWS, NK, KSUB)
        carry = carry + jnp.einsum("rki,kgrc->gic", slices, pulled_wide, precision=highest)
        return carry, grad_cols.astype(jnp.bfloat16).reshape(ROWS, KIN)

    site_grad, corner_grad = lax.scan(backward, jnp.zeros((NG, KSUB, CHIS), jnp.float32),
                                      jnp.arange(NSEC, dtype=jnp.int32))
    return (corner_new, corner_grad, site_grad)
```

```python
import functools
import jax
import jax.numpy as jnp
from jax import lax
from jax.experimental import pallas as pl
from jax.experimental.pallas import tpu as pltpu
from jax.sharding import PartitionSpec as P

F32 = jnp.float32
BF16 = jnp.bfloat16
NT = (((1,), (1,)), ((), ()))
VMEM = pl.BlockSpec(memory_space=pltpu.VMEM)
LIMIT = 40 * 1024 * 1024


def swap(value, axis, bit):
    size = lax.axis_size(axis)
    return lax.ppermute(value, axis, [(place, place ^ bit) for place in range(size)])


def total(*terms):
    acc = terms[0].astype(F32)
    for term in terms[1:]:
        acc = acc + term.astype(F32)
    return acc


def call(kernel, outs, args, scratch=(), flops=0):
    moved = sum(a.size * a.dtype.itemsize for a in args) + sum(
        a.size * a.dtype.itemsize for a in outs
    )
    return pl.pallas_call(
        kernel,
        out_shape=list(outs),
        in_specs=[VMEM] * len(args),
        out_specs=[VMEM] * len(outs),
        scratch_shapes=list(scratch),
        compiler_params=pltpu.CompilerParams(vmem_limit_bytes=LIMIT),
        cost_estimate=pl.CostEstimate(flops=flops, bytes_accessed=moved, transcendentals=0),
    )(*args)


def count_of(table, index, height, width):
    row = table[pl.ds(index, 1), :]
    wide = jnp.concatenate([row] * (width // row.shape[1]), axis=1)
    return jnp.broadcast_to(wide, (height, width))


def forward_kernel(owners, subs, blocks, x_ref, y_ref, site_ref, table_ref, *outs):
    rows, chi = outs[0].shape
    width = site_ref.shape[1]
    stacked = jnp.concatenate(
        [ref[:, sub * width : (sub + 1) * width] for ref in (x_ref, y_ref) for sub in range(subs)],
        axis=0,
    )
    accs = [jnp.zeros((rows, chi), F32) for _ in range(owners)]
    for block in range(0, blocks, 2):
        pair = jnp.concatenate([site_ref[block], site_ref[block + 1]], axis=1)
        product = jnp.dot(stacked, pair, preferred_element_type=F32)
        for sub in range(2 * subs):
            for offset in range(2):
                piece = product[sub * rows : (sub + 1) * rows, offset * chi : (offset + 1) * chi]
                for owner in range(owners):
                    index = (owner * 2 * subs + sub) * blocks + block + offset
                    accs[owner] = accs[owner] + piece * count_of(table_ref, index, rows, chi)
    for owner in range(owners):
        outs[owner][...] = accs[owner].astype(outs[owner].dtype)


def pulled_of(grads, table_ref, owners, subs, blocks, sub, block):
    value = None
    for owner in range(owners):
        index = (owner * 2 * subs + sub) * blocks + block
        term = grads[owner] * count_of(table_ref, index, *grads[owner].shape)
        value = term if value is None else value + term
    return value.astype(BF16)


def site_kernel(
    owners, subs, blocks, mine, place_ref, x_ref, y_ref, table_ref, *refs
):
    grads = [ref[...].astype(F32) for ref in refs[:owners]]
    acc, outs = refs[-1], refs[owners:-1]
    chi = grads[0].shape[0]
    width = acc.shape[1]
    for sub in range(2 * subs):
        source = x_ref if sub < subs else y_ref
        low = (sub % subs) * width
        left = jnp.concatenate(
            [
                pulled_of_dyn(grads, table_ref, owners, subs, blocks, sub, place_ref[0] + at)
                for at in range(mine)
            ],
            axis=0,
        )
        product = jnp.dot(left, source[:, low : low + width], preferred_element_type=F32)
        if sub == 0:
            acc[...] = product
        else:
            acc[...] += product
    if len(outs) == 1:
        outs[0][...] = acc[...]
        return
    half = mine // 2
    chunk = width // owners
    sends, kept, crossing, staying = outs[: owners - 1], outs[owners - 1], outs[-2], outs[-1]
    share = crossing.shape[1]
    for rel in range(owners):
        lanes = pl.ds(pl.multiple_of(place_ref[1 + rel] * chunk, chunk), chunk)
        out = kept if rel == 0 else sends[rel - 1]
        out[...] = acc[: half * chi, lanes].astype(out.dtype)
        for out, first in ((crossing, place_ref[owners + 2]), (staying, place_ref[owners + 1])):
            rows = pl.ds(pl.multiple_of(half * chi + first * share, share), share)
            out[rel] = acc[rows, lanes].astype(out.dtype)


def pulled_of_dyn(grads, table_ref, owners, subs, blocks, sub, block):
    value = None
    for owner in range(owners):
        index = (owner * 2 * subs + sub) * blocks + block
        term = grads[owner] * count_of(table_ref, index, *grads[owner].shape)
        value = term if value is None else value + term
    return value.astype(BF16)


def corner_kernel(owners, subs, blocks, site_ref, table_ref, *refs):
    grads = [ref[...].astype(F32).T for ref in refs[:owners]]
    out = refs[owners]
    rows = grads[0].shape[0]
    width = site_ref.shape[1]
    wide = jnp.concatenate([site_ref[block] for block in range(blocks)], axis=1)
    for sub in range(subs):
        left = jnp.concatenate(
            [pulled_of(grads, table_ref, owners, subs, blocks, sub, block) for block in range(blocks)],
            axis=1,
        )
        value = lax.dot_general(left, wide, NT, preferred_element_type=F32)
        out[:, sub * width : (sub + 1) * width] = value.astype(out.dtype)


def per_device(corner, site, projector, cotangent, sector_dim, pair_dest, pair_sub, pair_site):
    owners = lax.axis_size("sector")
    sides = lax.axis_size("block")
    me, side, rep = lax.axis_index("sector"), lax.axis_index("block"), lax.axis_index("rep")
    blocks, width, chi = site.shape
    rows = corner.shape[1]
    subs = corner.shape[2] // width
    direct = owners <= 4 and sides == 2
    flat = corner[0]

    other = swap(flat, "rep", 1)
    pairs = jnp.stack([pair_dest, pair_sub, pair_site])
    far = swap(pairs, "rep", 1)

    live = (jnp.arange(chi, dtype=jnp.int32) < sector_dim[0]).astype(BF16)
    grad = lax.dot_general(
        projector[0], cotangent[0] * live, NT, preferred_element_type=F32
    ).astype(BF16)
    if direct:
        grads = [grad] + [swap(grad, "sector", bit) for bit in range(1, owners)]
    else:
        shared = lax.all_gather(grad, "sector", axis=0)
        grads = [shared[owner] for owner in range(owners)]

    def rows_of(lists, first):
        dest = lists[0] ^ me if direct else lists[0]
        return (dest * 2 * subs + first + lists[1]) * blocks + lists[2]

    index = jnp.concatenate([rows_of(pairs, 0), rows_of(far, subs)])
    hits = (
        jnp.arange(owners * 2 * subs * blocks, dtype=jnp.int32)[:, None] == index[None, :]
    ).astype(BF16)
    table = jnp.dot(hits, jnp.ones((index.shape[0], 128), BF16), preferred_element_type=F32)

    part = rows // 2
    mine_x = lax.dynamic_slice_in_dim(flat, rep * part, part, 0)
    other_x = lax.dynamic_slice_in_dim(other, rep * part, part, 0)
    partials = call(
        functools.partial(forward_kernel, owners, subs, blocks),
        [jax.ShapeDtypeStruct((part, chi), BF16)] * owners,
        [mine_x, other_x, site, table],
        flops=4 * subs * part * width * chi * blocks,
    )
    if direct:
        arrived = [partials[0]] + [
            swap(partials[bit], "sector", bit) for bit in range(1, owners)
        ]
    else:
        arrived = list(
            lax.all_to_all(jnp.stack(partials), "sector", split_axis=0, concat_axis=0, tiled=True)
        )
    enlarged = total(*arrived).astype(BF16)
    projected = jnp.dot(enlarged, projector[0], preferred_element_type=F32)
    projected = (projected * live.astype(F32)).astype(BF16)

    mine = blocks // 2
    half = mine // 2
    place = jnp.stack(
        [rep * mine] + [me ^ rel for rel in range(owners)] + [side, 1 - side]
    ).astype(jnp.int32)
    if direct:
        chunk = width // owners
        share = half * chi // sides
        outs = [jax.ShapeDtypeStruct((half * chi, chunk), BF16)] * owners
        outs += [jax.ShapeDtypeStruct((owners, share, chunk), BF16)] * 2
    else:
        outs = [jax.ShapeDtypeStruct((mine * chi, width), F32)]
    args = [place, flat, other, table] + grads
    pieces = pl.pallas_call(
        functools.partial(site_kernel, owners, subs, blocks, mine),
        out_shape=outs,
        in_specs=[pl.BlockSpec(memory_space=pltpu.SMEM)] + [VMEM] * (len(args) - 1),
        out_specs=[VMEM] * len(outs),
        scratch_shapes=[pltpu.VMEM((mine * chi, width), F32)],
        compiler_params=pltpu.CompilerParams(vmem_limit_bytes=LIMIT),
        cost_estimate=pl.CostEstimate(
            flops=4 * subs * rows * width * chi * mine, bytes_accessed=1 << 22, transcendentals=0
        ),
    )(*args)
    if direct:
        crossing, staying = pieces[owners], pieces[owners + 1]
        crossed = swap(crossing, "block", 1)
        first = [pieces[owners - 1]] + [
            swap(pieces[bit - 1], "sector", bit) for bit in range(owners - 1, 0, -1)
        ]
        merged = total(staying, crossed).astype(BF16)
        second = [merged[0]] + [swap(merged[bit], "sector", bit) for bit in range(owners - 1, 0, -1)]
        upper = total(*first).astype(BF16)
        upper = total(upper, swap(upper, "block", 1)).astype(BF16)
        lower = total(*second).astype(BF16)
        beside = swap(lower, "block", 1)
        lower = jnp.where(
            side == 0, jnp.concatenate([lower, beside]), jnp.concatenate([beside, lower])
        )
        own = jnp.concatenate([upper, lower, projected], axis=0)
        there = swap(own, "rep", 1)
        both = jnp.where(rep == 0, jnp.stack([own, there]), jnp.stack([there, own]))
        site_grad = both[:, : mine * chi].reshape(blocks, chi, chunk).swapaxes(1, 2).astype(F32)
        corner_new = both[:, mine * chi :].reshape(1, rows, chi)
    else:
        term = pieces[0].astype(BF16).reshape(mine, chi, width)
        term = lax.psum_scatter(term, "sector", scatter_dimension=2, tiled=True)
        term = lax.psum(term, "block")
        gathered = lax.all_gather(term, "rep", axis=0, tiled=True)
        site_grad = gathered.swapaxes(1, 2).astype(F32)
        corner_new = lax.all_gather(projected, "rep", axis=0, tiled=True)[None]

    corner_grad = call(
        functools.partial(corner_kernel, owners, subs, blocks),
        [jax.ShapeDtypeStruct((rows, subs * width), BF16)],
        [site, table] + grads,
        flops=2 * subs * rows * width * chi * blocks,
    )[0][None]
    return (corner_new, corner_grad, site_grad)


def solution(mesh):
    in_specs = (
        P(("groups", "sector"), "block", "rep"),
        P("groups", None, None),
        P(("groups", "sector"), None, None),
        P(("groups", "sector"), "block", None),
        P(("groups", "sector")),
        P(("groups", "sector", "rep")),
        P(("groups", "sector", "rep")),
        P(("groups", "sector", "rep")),
    )
    out_specs = (
        P(("groups", "sector"), "block", None),
        P(("groups", "sector"), "block", "rep"),
        P("groups", "sector", None),
    )
    return jax.shard_map(
        per_device, mesh=mesh, in_specs=in_specs, out_specs=out_specs, check_vma=False
    )
```

```python
import functools
import jax
import jax.numpy as jnp
from jax import lax
from jax.experimental import pallas as pl
from jax.experimental.pallas import tpu as pltpu
from jax.sharding import PartitionSpec as P

F32 = jnp.float32
BF16 = jnp.bfloat16
NT = (((1,), (1,)), ((), ()))
LIMIT = 24 * 1024 * 1024


def swap(value, axis, bit):
    size = lax.axis_size(axis)
    return lax.ppermute(value, axis, [(place, place ^ bit) for place in range(size)])


def total(*terms):
    acc = terms[0].astype(F32)
    for term in terms[1:]:
        acc = acc + term.astype(F32)
    return acc


def call(kernel, outs, args, scratch=(), flops=0, far=0):
    moved = sum(a.size * a.dtype.itemsize for a in args) + sum(
        a.size * a.dtype.itemsize for a in outs
    )
    scalars = pl.BlockSpec(memory_space=pltpu.SMEM)
    vectors = pl.BlockSpec(memory_space=pltpu.VMEM)
    return pl.pallas_call(
        kernel,
        out_shape=list(outs),
        in_specs=[pl.BlockSpec(memory_space=pltpu.HBM)] * far
        + [scalars if a.ndim == 1 else vectors for a in args[far:]],
        out_specs=[vectors] * len(outs),
        scratch_shapes=list(scratch),
        compiler_params=pltpu.CompilerParams(vmem_limit_bytes=LIMIT),
        cost_estimate=pl.CostEstimate(flops=flops, bytes_accessed=moved, transcendentals=0),
    )(*[pltpu.with_memory_space_constraint(a, pltpu.HBM) for a in args[:far]], *args[far:])


def start_all(arrived, *pairs):
    copies = [
        pltpu.make_async_copy(source, target, arrived.at[at])
        for at, (source, target) in enumerate(pairs)
    ]
    for copy in copies:
        copy.start()
    return copies


def count_table(pairs_ref, table_ref):
    places, lanes = table_ref.shape
    pairs = pairs_ref.shape[1]
    hits = lax.broadcasted_iota(jnp.int32, (places, pairs), 0) == pairs_ref[...]
    table_ref[...] = jnp.dot(
        jnp.where(hits, 1.0, 0.0).astype(BF16),
        jnp.ones((pairs, lanes), BF16),
        preferred_element_type=F32,
    )


def count_of(table_ref, index, height, width):
    row = table_ref[pl.ds(index, 1), :]
    wide = jnp.concatenate([row] * (width // row.shape[1]), axis=1)
    return jnp.broadcast_to(wide, (height, width))


def grad_kernel(
    owners, subs, blocks, projector_hbm, cotangent_hbm, dest_hbm, sub_hbm, site_hbm, dim_ref,
    out_ref, live_ref, combo_ref, projector_ref, cotangent_ref, lists_ref, arrived
):
    copies = start_all(
        arrived,
        (cotangent_hbm, cotangent_ref),
        (projector_hbm, projector_ref),
        (dest_hbm, lists_ref.at[0]),
        (sub_hbm, lists_ref.at[1]),
        (site_hbm, lists_ref.at[2]),
    )
    for copy in copies:
        copy.wait()
    combo_ref[...] = (lists_ref[0] * subs + lists_ref[1]) * blocks + lists_ref[2]
    lane = lax.broadcasted_iota(jnp.int32, projector_ref.shape, 1)
    live = jnp.where(lane < dim_ref[0], 1.0, 0.0)
    live_ref[...] = live[: live_ref.shape[0]]
    out_ref[...] = lax.dot_general(
        (projector_ref[...].astype(F32) * live).astype(BF16),
        cotangent_ref[...],
        NT,
        preferred_element_type=F32,
    ).astype(out_ref.dtype)


def forward_kernel(owners, subs, blocks, x_hbm, site_hbm, place_ref, own_ref, far_ref, y_ref, *refs):
    outs, (x_ref, site_ref, table_ref, arrived) = refs[:owners], refs[owners:]
    rows, chi = outs[0].shape
    width = site_ref.shape[1]
    step = 2
    copies = start_all(
        arrived,
        *[
            (site_hbm.at[block : block + step], site_ref.at[block : block + step])
            for block in range(0, blocks, step)
        ],
        (x_hbm, x_ref),
    )
    places = table_ref.shape[0] // 2
    count_table(own_ref, table_ref.at[:places])
    count_table(far_ref, table_ref.at[places:])
    mine = pl.ds(pl.multiple_of(place_ref[owners + 3], rows), rows)
    copies[0].wait()
    copies[-1].wait()
    stacked = jnp.concatenate(
        [ref[mine, sub * width : (sub + 1) * width] for ref in (x_ref, y_ref) for sub in range(subs)],
        axis=0,
    )
    accs = [jnp.zeros((rows, chi), F32) for _ in range(owners)]
    for block in range(0, blocks, step):
        if block:
            copies[block // step].wait()
        pair = jnp.concatenate([site_ref[block + offset] for offset in range(step)], axis=1)
        product = jnp.dot(stacked, pair, preferred_element_type=F32)
        for sub in range(2 * subs):
            for offset in range(step):
                piece = product[sub * rows : (sub + 1) * rows, offset * chi : (offset + 1) * chi]
                for owner in range(owners):
                    index = place_of(owners, subs, blocks, owner, sub, block + offset)
                    accs[owner] = accs[owner] + piece * count_of(table_ref, index, rows, chi)
    for owner in range(owners):
        outs[owner][...] = accs[owner].astype(outs[owner].dtype)


def place_of(owners, subs, blocks, owner, sub, block):
    return ((sub // subs * owners + owner) * subs + sub % subs) * blocks + block


def pulled_of(grads, table_ref, owners, subs, blocks, sub, block):
    value = None
    for owner, grad in enumerate(grads):
        index = place_of(owners, subs, blocks, owner, sub, block)
        term = grad * count_of(table_ref, index, *grad.shape)
        value = term if value is None else value + term
    return value.astype(BF16)


def site_kernel(owners, subs, blocks, taken, first, place_ref, table_ref, x_ref, y_ref, *refs):
    partials, refs = refs[:owners], refs[owners:]
    grads = [ref[...].astype(F32) for ref in refs[:owners]]
    outs, acc = refs[owners:-1], refs[-1]
    chi = grads[0].shape[0]
    width = acc.shape[1]
    for sub in range(2 * subs):
        source = x_ref if sub < subs else y_ref
        low = (sub % subs) * width
        left = [
            pulled_of(grads, table_ref, owners, subs, blocks, sub, place_ref[0] + at)
            for at in range(taken)
        ]
        product = jnp.dot(
            jnp.concatenate(left, axis=0), source[:, low : low + width], preferred_element_type=F32
        )
        if sub == 0:
            acc[...] = product
        else:
            acc[...] += product
    if len(outs) == 1:
        outs[0][...] = acc[...]
        return
    chunk = width // owners
    straight = first * chi
    crossing, staying = outs[owners:]
    share = crossing.shape[1]
    for rel in range(owners):
        lanes = pl.ds(pl.multiple_of(place_ref[1 + rel] * chunk, chunk), chunk)
        outs[rel][:straight] = acc[:straight, lanes].astype(outs[rel].dtype)
        outs[rel][straight:] = partials[rel][...].astype(outs[rel].dtype)
        for out, slot in ((crossing, 1), (staying, 0)):
            rows = pl.ds(pl.multiple_of(straight + place_ref[1 + owners + slot] * share, share), share)
            out[rel] = acc[rows, lanes].astype(out.dtype)


def corner_kernel(owners, subs, blocks, site_ref, table_ref, *refs):
    grads = [ref[...].astype(F32).T for ref in refs[:owners]]
    out = refs[owners]
    width = site_ref.shape[1]
    wide = jnp.concatenate([site_ref[block] for block in range(blocks)], axis=1)
    for sub in range(subs):
        left = jnp.concatenate(
            [pulled_of(grads, table_ref, owners, subs, blocks, sub, block) for block in range(blocks)],
            axis=1,
        )
        value = lax.dot_general(left, wide, NT, preferred_element_type=F32)
        out[:, sub * width : (sub + 1) * width] = value.astype(out.dtype)


def per_device(corner, site, projector, cotangent, sector_dim, pair_dest, pair_sub, pair_site):
    owners = lax.axis_size("sector")
    sides = lax.axis_size("block")
    me, side, rep = lax.axis_index("sector"), lax.axis_index("block"), lax.axis_index("rep")
    blocks, width, chi = site.shape
    rows = corner.shape[1]
    subs = corner.shape[2] // width
    pairs = pair_dest.shape[0]
    direct = owners * chi == width and sides == 2
    flat = corner[0]
    mine = blocks // 2
    first = mine // 4
    part = rows // 2
    chunk = width // owners
    places = owners * subs * blocks
    shape = jax.ShapeDtypeStruct
    place = jnp.stack(
        [rep * mine]
        + [me ^ rel for rel in range(owners)]
        + [side, 1 - side, rep * part, (1 - rep) * part]
    ).astype(jnp.int32)

    other = swap(flat, "rep", 1)
    def placed(value):
        if direct:
            stride = subs * blocks
            value = (value // stride ^ me) * stride + value % stride
        return value

    sizes = (owners, subs, blocks)
    lists = [value.reshape(1, pairs) for value in (pair_dest, pair_sub, pair_site)]
    grad, live, combo = call(
        functools.partial(grad_kernel, *sizes),
        [shape((chi, rows), BF16), shape((8, chi), F32), shape((1, pairs), jnp.int32)],
        [projector[0], cotangent[0], *lists, sector_dim],
        [
            pltpu.VMEM((chi, chi), BF16),
            pltpu.VMEM((rows, chi), BF16),
            pltpu.VMEM((3, 1, pairs), jnp.int32),
            pltpu.SemaphoreType.DMA((5,)),
        ],
        far=5,
    )
    far = swap(combo, "rep", 1)
    if direct:
        grads = [grad] + [swap(grad, "sector", bit) for bit in range(1, owners)]
    else:
        shared = lax.all_gather(grad, "sector", axis=0)
        grads = [shared[owner] for owner in range(owners)]

    *partials, near, blocks_near, table = call(
        functools.partial(forward_kernel, *sizes),
        [shape((part, chi), BF16)] * owners
        + [shape(flat.shape, BF16), shape(site.shape, BF16), shape((2 * places, 128), F32)],
        [flat, site, place, placed(combo), placed(far), other],
        [pltpu.SemaphoreType.DMA((1 + blocks // 2,))],
        flops=4 * subs * rows * width * chi * blocks,
        far=2,
    )

    def project(enlarged):
        value = jnp.dot(enlarged.astype(BF16), projector[0], preferred_element_type=F32)
        return (value * live[:1]).astype(BF16)

    def corner_term(after):
        args = lax.optimization_barrier(((blocks_near, table, *grads), after))[0]
        return call(
            functools.partial(corner_kernel, *sizes),
            [shape((rows, subs * width), BF16)],
            list(args),
            flops=2 * subs * rows * width * chi * owners,
        )[0][None]

    if direct:
        share = (mine - first) * chi // sides
        height = first * chi + part
        outs = [shape((height, chunk), F32)] + [shape((height, chunk), BF16)] * (owners - 1)
        outs += [shape((owners, share, chunk), BF16), shape((owners, share, chunk), F32)]
    else:
        outs = [shape((mine * chi, width), F32)]
    pieces = call(
        functools.partial(site_kernel, *sizes, mine, first),
        outs,
        [place, table, near, other, *partials, *grads],
        [pltpu.VMEM((mine * chi, width), F32)],
        flops=4 * subs * rows * width * chi * mine,
    )
    if direct:
        bits = range(owners - 1, 0, -1)
        straight = first * chi
        crossed = swap(pieces[owners], "block", 1)
        direct_sums = [pieces[0]] + [swap(pieces[bit], "sector", bit) for bit in bits]
        merged = total(pieces[owners + 1], crossed)
        sent = merged.astype(BF16)
        shared_sums = [merged[0]] + [swap(sent[bit], "sector", bit) for bit in bits]
        upper = total(*direct_sums)
        projected = project(upper[straight:])
        upper = upper[:straight]
        corner_grad = corner_term(upper)
        lower = total(*shared_sums)
        both = jnp.concatenate([upper, lower]).astype(BF16)
        both, corner_grad = lax.optimization_barrier((both, corner_grad))
        beside = swap(both, "block", 1)
        upper = total(upper, beside[:straight]).astype(BF16)
        lower, under = both[straight:], beside[straight:]
        own = jnp.concatenate(
            [upper, jnp.where(side == 0, lower, under), jnp.where(side == 0, under, lower)]
        )
        projected = [projected, swap(projected, "rep", 1)]
        there = swap(own, "rep", 1)

        def ordered(pair):
            return jnp.where(rep == 0, jnp.stack(pair), jnp.stack(pair[::-1]))

        corner_new = ordered(projected).reshape(1, rows, chi)
        site_grad = ordered([own, there]).reshape(blocks, chi, chunk).swapaxes(1, 2).astype(F32)
    else:
        term = pieces[0].astype(BF16).reshape(mine, chi, width)
        term = lax.psum_scatter(term, "sector", scatter_dimension=2, tiled=True)
        term = lax.psum(term, "block")
        site_grad = lax.all_gather(term, "rep", axis=0, tiled=True).swapaxes(1, 2).astype(F32)
        arrived = lax.all_to_all(
            jnp.stack(partials), "sector", split_axis=0, concat_axis=0, tiled=True
        )
        projected = project(jnp.sum(arrived.astype(F32), axis=0))
        corner_new = lax.all_gather(projected, "rep", axis=0, tiled=True)[None]
        corner_grad = corner_term(term)
    return (corner_new, corner_grad, site_grad)


def solution(mesh):
    in_specs = (
        P(("groups", "sector"), "block", "rep"),
        P("groups", None, None),
        P(("groups", "sector"), None, None),
        P(("groups", "sector"), "block", None),
        P(("groups", "sector")),
        P(("groups", "sector", "rep")),
        P(("groups", "sector", "rep")),
        P(("groups", "sector", "rep")),
    )
    out_specs = (
        P(("groups", "sector"), "block", None),
        P(("groups", "sector"), "block", "rep"),
        P("groups", "sector", None),
    )
    return jax.shard_map(
        per_device, mesh=mesh, in_specs=in_specs, out_specs=out_specs, check_vma=False
    )
```

```python
import functools
import jax
import jax.numpy as jnp
from jax import lax
from jax.experimental import pallas as pl
from jax.experimental.pallas import tpu as pltpu
from jax.sharding import PartitionSpec as P

F32 = jnp.float32
BF16 = jnp.bfloat16
NT = (((1,), (1,)), ((), ()))
LIMIT = 28 * 1024 * 1024


def swap(value, axis, bit):
    size = lax.axis_size(axis)
    return lax.ppermute(value, axis, [(place, place ^ bit) for place in range(size)])


def total(*terms):
    acc = terms[0].astype(F32)
    for term in terms[1:]:
        acc = acc + term.astype(F32)
    return acc


def call(kernel, outs, args, scratch=(), flops=0, after=()):
    args = [*args, *after]
    moved = sum(a.size * a.dtype.itemsize for a in args) + sum(
        a.size * a.dtype.itemsize for a in outs
    )
    scalars = pl.BlockSpec(memory_space=pltpu.SMEM)
    vectors = pl.BlockSpec(memory_space=pltpu.VMEM)
    return pl.pallas_call(
        kernel,
        out_shape=list(outs),
        in_specs=[scalars if a.ndim == 1 else vectors for a in args[: len(args) - len(after)]]
        + [pl.BlockSpec(memory_space=pl.ANY)] * len(after),
        out_specs=[vectors] * len(outs),
        scratch_shapes=list(scratch),
        compiler_params=pltpu.CompilerParams(vmem_limit_bytes=LIMIT),
        cost_estimate=pl.CostEstimate(flops=flops if flops >> 34 else 0, bytes_accessed=moved, transcendentals=0),
    )(*args)


def count_of(table_ref, index, height, width):
    row = table_ref[pl.ds(index, 1), :]
    wide = jnp.concatenate([row] * (width // row.shape[1]), axis=1)
    return jnp.broadcast_to(wide, (height, width))


def lanes_kernel(out_ref):
    out_ref[...] = lax.broadcasted_iota(jnp.int32, out_ref.shape, 1)


def grad_kernel(dim_ref, lanes_ref, projector_ref, cotangent_ref, out_ref, live_ref):
    live = jnp.where(lanes_ref[...] < dim_ref[0], 1.0, 0.0)
    live_ref[...] = live
    masked = projector_ref[...].astype(F32) * live[:1]
    out_ref[...] = lax.dot_general(
        masked.astype(BF16), cotangent_ref[...], NT, preferred_element_type=F32
    ).astype(out_ref.dtype)


def forward_kernel(owners, subs, blocks, table_ref, x_ref, site_ref, keep_ref, send_ref, product_ref, sum_ref):
    rows, chi = keep_ref.shape[1:]
    width = site_ref.shape[1]
    step, tile = 2, 32
    rep = lax.axis_index("rep")
    stacked = jnp.concatenate(
        [
            x_ref[pl.ds(pl.multiple_of(half * rows, rows), rows), sub * width : (sub + 1) * width]
            for half in (1 - rep, rep)
            for sub in range(subs)
        ],
        axis=0,
    )
    for low in range(0, blocks, step):
        pair = jnp.concatenate(
            [site_ref[block_at(blocks, low + offset)] for offset in range(step)], axis=1
        )
        product_ref[low // step % 2] = jnp.dot(stacked, pair, preferred_element_type=F32)

        def add(at, low=low):
            for half, out_ref in ((1, keep_ref), (0, sum_ref)):
                pieces = [
                    product_ref[
                        low // step % 2,
                        pl.ds((half * subs + sub) * rows + at, tile),
                        offset * chi : (offset + 1) * chi,
                    ]
                    for sub in range(subs)
                    for offset in range(step)
                ]
                for owner in range(owners):
                    value = None
                    for sub in range(subs):
                        for offset in range(step):
                            index = (owner * subs + sub) * blocks + low + offset
                            term = pieces[sub * step + offset] * count_of(table_ref, index, tile, chi)
                            value = term if value is None else value + term
                    if low:
                        value = value + out_ref[owner, pl.ds(at, tile)]
                    out_ref[owner, pl.ds(at, tile)] = value

        if owners <= 4:
            for at in range(0, rows, tile):
                add(at)
        else:
            pl.loop(0, rows, step=tile)(lambda at: add(pl.multiple_of(at, tile)))
    send_ref[...] = sum_ref[...].astype(send_ref.dtype)


def site_kernel(
    owners, subs, blocks, taken, first, own_table, far_table, x_ref, y_ref, keep_ref, got_ref, *refs
):
    grads, outs, left_ref = refs[:owners], refs[owners:-1], refs[-1]
    chi, rows = grads[0].shape
    width = x_ref.shape[1] // subs
    cut = len(outs) > 1
    whole = [ref[...].astype(F32) for ref in grads]
    parts = [(at, whole) for at in range(first if cut else taken)]
    if cut:
        crossing, staying = outs[owners:]
        share = crossing.shape[1] // (taken - first)
        side = lax.axis_index("block")
        for slot in (1 - side, side):
            mine = pl.ds(pl.multiple_of(slot * share, share), share)
            shared = [ref[mine, :].astype(F32) for ref in grads]
            parts += [(at, shared) for at in range(first, taken)]
    tables = [own_table, far_table]
    for sub in range(2 * subs):
        low = 0
        for at, values in parts:
            height = values[0].shape[0]
            left_ref[low : low + height, sub * rows : (sub + 1) * rows] = pulled_of(
                values, tables[sub // subs], subs, blocks, sub % subs, at
            )
            low += height
    chunk = width // owners
    step = max(1, 256 // chunk) if cut else owners
    for rel in range(0, owners, step):
        columns = []
        for ref in (x_ref, y_ref):
            for sub in range(subs):
                pieces = [
                    ref[:, pl.ds(pl.multiple_of(sub * width + (lax.axis_index("sector") ^ at) * chunk, chunk), chunk)]
                    for at in range(rel, rel + step)
                ]
                columns.append(
                    jnp.concatenate(pieces, axis=1) if cut else ref[:, sub * width : (sub + 1) * width]
                )
        product = jnp.dot(
            left_ref[...], jnp.concatenate(columns, axis=0), preferred_element_type=F32
        )
        if not cut:
            outs[0][...] = product
            return
        straight, middle = first * chi, first * chi + crossing.shape[1]
        for at in range(step):
            lanes = slice(at * chunk, (at + 1) * chunk)
            out = outs[rel + at]
            partial = keep_ref[rel + at] + got_ref[rel + at].astype(F32)
            out[:straight] = product[:straight, lanes].astype(out.dtype)
            out[straight:] = partial.astype(BF16).astype(out.dtype)
            crossing[rel + at] = product[straight:middle, lanes].astype(crossing.dtype)
            staying[rel + at] = product[middle:, lanes].astype(staying.dtype)


def block_at(blocks, at):
    return lax.rem(lax.axis_index("rep") * (blocks // 2) + at, blocks)


def pulled_of(grads, table_ref, subs, blocks, sub, block):
    value = None
    for owner, grad in enumerate(grads):
        index = (owner * subs + sub) * blocks + block
        term = grad * count_of(table_ref, index, *grad.shape)
        value = term if value is None else value + term
    return value.astype(BF16)


def sum_kernel(count, *refs):
    out_ref, rest_ref = refs[-2:]
    upper, lower = total(*[ref[...] for ref in refs[:count]]), total(*[ref[...] for ref in refs[count : 2 * count]])
    straight = out_ref.shape[0] - lower.shape[0]
    out_ref[:straight] = upper[:straight].astype(out_ref.dtype)
    out_ref[straight:] = lower.astype(out_ref.dtype)
    rest_ref[...] = upper[straight:].astype(rest_ref.dtype)


def corner_kernel(owners, subs, blocks, site_ref, table_ref, *refs):
    grads = [ref[...].astype(F32).T for ref in refs[:owners]]
    out, token = refs[-2:]
    token[...] = jnp.zeros(token.shape, token.dtype)
    width = site_ref.shape[1]
    wide = jnp.concatenate(
        [site_ref[block_at(blocks, block)] for block in range(blocks)], axis=1
    )
    for sub in range(subs):
        left = jnp.concatenate(
            [pulled_of(grads, table_ref, subs, blocks, sub, block) for block in range(blocks)],
            axis=1,
        )
        value = lax.dot_general(left, wide, NT, preferred_element_type=F32)
        out[:, sub * width : (sub + 1) * width] = value.astype(out.dtype)


def per_device(corner, site, projector, cotangent, sector_dim, pair_dest, pair_sub, pair_site):
    owners = lax.axis_size("sector")
    sides = lax.axis_size("block")
    me, side, rep = lax.axis_index("sector"), lax.axis_index("block"), lax.axis_index("rep")
    blocks, width, chi = site.shape
    rows = corner.shape[1]
    subs = corner.shape[2] // width
    pairs = pair_dest.shape[0]
    direct = owners * chi == width and sides == 2 and blocks >= 8
    flat = corner[0]
    mine = blocks // 2
    first = mine // 2
    part = rows // 2
    chunk = width // owners
    places = owners * subs * blocks
    shape = jax.ShapeDtypeStruct
    other = swap(flat, "rep", 1)
    def table_of(value):
        if direct:
            stride = subs * blocks
            value = (value // stride ^ me) * stride + value % stride
        value = value // blocks * blocks + (value + rep * mine) % blocks
        hits = (jnp.arange(places, dtype=jnp.int32)[:, None] == value[None, :]).astype(BF16)
        return jnp.dot(hits, jnp.ones((pairs, 128), BF16), preferred_element_type=F32)

    sizes = (owners, subs, blocks)
    combo = (pair_dest * subs + pair_sub) * blocks + pair_site
    lanes = call(lanes_kernel, [shape((8, chi), jnp.int32)], [], flops=1 << 34)[0]
    grad, live = call(
        grad_kernel,
        [shape((chi, rows), BF16), shape((8, chi), F32)],
        [sector_dim, lanes, projector[0], cotangent[0]],
    )
    far = swap(combo, "rep", 1)
    if direct:
        grads = [grad] + [swap(grad, "sector", bit) for bit in range(1, owners)]
    else:
        shared = lax.all_gather(grad, "sector", axis=0)
        grads = [shared[owner] for owner in range(owners)]

    near, distant = table_of(combo), table_of(far)
    keep, send = call(
        functools.partial(forward_kernel, *sizes),
        [shape((owners, part, chi), F32), shape((owners, part, chi), BF16)],
        [near, flat, site],
        [
            pltpu.VMEM((2, 2 * part * subs, 2 * chi), F32),
            pltpu.VMEM((owners, part, chi), F32),
        ],
        flops=4 * subs * rows * width * chi * blocks,
    )
    got = swap(send, "rep", 1)

    def project(enlarged):
        value = jnp.dot(enlarged.astype(BF16), projector[0], preferred_element_type=F32)
        return (value * live[:1]).astype(BF16)

    def corner_term(after):
        return call(
            functools.partial(corner_kernel, *sizes),
            [shape((rows, subs * width), BF16), shape((8, chi), F32)],
            [site, near, *grads],
            flops=2 * subs * rows * width * chi * owners,
            after=[after],
        )

    if direct:
        share = (mine - first) * chi // sides
        height = first * chi + part
        outs = [shape((height, chunk), F32)] + [shape((height, chunk), BF16)] * (owners - 1)
        outs += [shape((owners, share, chunk), BF16), shape((owners, share, chunk), F32)]
    else:
        outs = [shape((mine * chi, width), F32)]
    pieces = call(
        functools.partial(site_kernel, *sizes, mine, first),
        outs,
        [near, distant, flat, other, keep, got, *grads],
        [pltpu.VMEM((mine * chi, 2 * subs * rows), BF16)],
        flops=4 * subs * rows * width * chi * mine,
    )
    if direct:
        bits = range(owners - 1, 0, -1)
        straight = first * chi
        crossed = swap(pieces[owners], "block", 1)
        direct_sums = [pieces[0]] + [swap(pieces[bit], "sector", bit) for bit in bits]
        merged = total(pieces[owners + 1], crossed)
        sent = merged.astype(BF16)
        shared_sums = [merged[0]] + [swap(sent[bit], "sector", bit) for bit in bits]
        corner_grad, token = corner_term(sent)
        both, enlarged = call(
            functools.partial(sum_kernel, owners),
            [shape((straight + share, chunk), BF16), shape((part, chunk), BF16)],
            [*direct_sums, *shared_sums],
            after=[token],
        )
        projected = project(enlarged)
        beside = swap(both, "block", 1)
        upper = total(both[:straight], beside[:straight]).astype(BF16)
        lower, under = [
            value[straight:].reshape(mine - first, chi // sides, chunk) for value in (both, beside)
        ]
        lower = jnp.where(
            side == 0,
            jnp.concatenate([lower, under], axis=1),
            jnp.concatenate([under, lower], axis=1),
        )
        own = jnp.concatenate([upper, lower.reshape(share * sides, chunk)])
        projected = [projected, swap(projected, "rep", 1)]
        there = swap(own, "rep", 1)

        def ordered(pair):
            return jnp.where(rep == 0, jnp.stack(pair), jnp.stack(pair[::-1]))

        corner_new = ordered(projected).reshape(1, rows, chi)
        site_grad = ordered([own, there]).reshape(blocks, chi, chunk).swapaxes(1, 2).astype(F32)
    else:
        term = pieces[0].astype(BF16).reshape(mine, chi, width)
        term = lax.psum_scatter(term, "sector", scatter_dimension=2, tiled=True)
        term = lax.psum(term, "block")
        site_grad = lax.all_gather(term, "rep", axis=0, tiled=True).swapaxes(1, 2).astype(F32)
        partials = (keep + got.astype(F32)).astype(BF16)
        arrived = lax.all_to_all(partials, "sector", split_axis=0, concat_axis=0, tiled=True)
        projected = project(jnp.sum(arrived.astype(F32), axis=0))
        corner_new = lax.all_gather(projected, "rep", axis=0, tiled=True)[None]
        corner_grad = corner_term(term)[0]
    return (corner_new, corner_grad[None], site_grad)


def solution(mesh):
    in_specs = (
        P(("groups", "sector"), "block", "rep"),
        P("groups", None, None),
        P(("groups", "sector"), None, None),
        P(("groups", "sector"), "block", None),
        P(("groups", "sector")),
        P(("groups", "sector", "rep")),
        P(("groups", "sector", "rep")),
        P(("groups", "sector", "rep")),
    )
    out_specs = (
        P(("groups", "sector"), "block", None),
        P(("groups", "sector"), "block", "rep"),
        P("groups", "sector", None),
    )
    return jax.shard_map(
        per_device, mesh=mesh, in_specs=in_specs, out_specs=out_specs, check_vma=False
    )
```

```python
import functools
import jax
import jax.numpy as jnp
from jax import lax
from jax.experimental import pallas as pl
from jax.experimental.pallas import tpu as pltpu
from jax.sharding import PartitionSpec as P

F32 = jnp.float32
BF16 = jnp.bfloat16
NT = (((1,), (1,)), ((), ()))
LIMIT = 28 * 1024 * 1024


def swap(value, axis, bit):
    size = lax.axis_size(axis)
    return lax.ppermute(value, axis, [(place, place ^ bit) for place in range(size)])


def total(*terms):
    acc = terms[0].astype(F32)
    for term in terms[1:]:
        acc = acc + term.astype(F32)
    return acc


def call(kernel, outs, args, scratch=(), flops=0, after=(), stores=0):
    args = [*args, *after]
    moved = sum(a.size * a.dtype.itemsize for a in args) + sum(
        a.size * a.dtype.itemsize for a in outs
    )
    scalars = pl.BlockSpec(memory_space=pltpu.SMEM)
    vectors = pl.BlockSpec(memory_space=pltpu.VMEM)
    return pl.pallas_call(
        kernel,
        out_shape=list(outs),
        in_specs=[scalars if a.ndim == 1 else vectors for a in args[: len(args) - len(after)]]
        + [pl.BlockSpec(memory_space=pl.ANY)] * len(after),
        out_specs=[pl.BlockSpec(memory_space=pltpu.HBM)] * stores + [vectors] * (len(outs) - stores),
        scratch_shapes=list(scratch),
        compiler_params=pltpu.CompilerParams(vmem_limit_bytes=LIMIT),
        cost_estimate=pl.CostEstimate(flops=flops if flops >> 34 else 0, bytes_accessed=moved, transcendentals=0),
    )(*args)


def count_of(table_ref, index, height, width):
    row = table_ref[pl.ds(index, 1), :]
    wide = jnp.concatenate([row] * (width // row.shape[1]), axis=1)
    return jnp.broadcast_to(wide, (height, width))


def lanes_kernel(out_ref):
    out_ref[...] = lax.broadcasted_iota(jnp.int32, out_ref.shape, 1)


def grad_kernel(dim_ref, lanes_ref, projector_ref, cotangent_ref, out_ref, live_ref):
    live = jnp.where(lanes_ref[...] < dim_ref[0], 1.0, 0.0)
    live_ref[...] = live
    masked = projector_ref[...].astype(F32) * live[:1]
    out_ref[...] = lax.dot_general(
        masked.astype(BF16), cotangent_ref[...], NT, preferred_element_type=F32
    ).astype(out_ref.dtype)


def forward_kernel(owners, subs, blocks, table_ref, x_ref, site_ref, keep_ref, send_ref, product_ref, sum_ref):
    rows, chi = keep_ref.shape[1:]
    width = site_ref.shape[1]
    step, tile = 2, 32
    rep = lax.axis_index("rep")
    stacked = jnp.concatenate(
        [
            x_ref[pl.ds(pl.multiple_of(half * rows, rows), rows), sub * width : (sub + 1) * width]
            for half in (1 - rep, rep)
            for sub in range(subs)
        ],
        axis=0,
    )
    for low in range(0, blocks, step):
        pair = jnp.concatenate(
            [site_ref[block_at(blocks, low + offset)] for offset in range(step)], axis=1
        )
        product_ref[low // step % 2] = jnp.dot(stacked, pair, preferred_element_type=F32)

        def add(at, low=low):
            for half, out_ref in ((1, keep_ref), (0, sum_ref)):
                pieces = [
                    product_ref[
                        low // step % 2,
                        pl.ds((half * subs + sub) * rows + at, tile),
                        offset * chi : (offset + 1) * chi,
                    ]
                    for sub in range(subs)
                    for offset in range(step)
                ]
                for owner in range(owners):
                    value = None
                    for sub in range(subs):
                        for offset in range(step):
                            index = (owner * subs + sub) * blocks + low + offset
                            term = pieces[sub * step + offset] * count_of(table_ref, index, tile, chi)
                            value = term if value is None else value + term
                    if low:
                        value = value + out_ref[owner, pl.ds(at, tile)]
                    out_ref[owner, pl.ds(at, tile)] = value

        if owners <= 4:
            for at in range(0, rows, tile):
                add(at)
        else:
            pl.loop(0, rows, step=tile)(lambda at: add(pl.multiple_of(at, tile)))
    send_ref[...] = sum_ref[...].astype(send_ref.dtype)


def site_kernel(
    owners, subs, blocks, taken, first, own_table, far_table, x_ref, y_ref, keep_ref, got_ref, *refs
):
    grads, outs, left_ref = refs[:owners], refs[owners:-1], refs[-1]
    chi, rows = grads[0].shape
    width = x_ref.shape[1] // subs
    cut = len(outs) > 1
    whole = [ref[...].astype(F32) for ref in grads]
    parts = [(at, whole) for at in range(first if cut else taken)]
    if cut:
        crossing, staying = outs[owners:]
        share = crossing.shape[1] // (taken - first)
        side = lax.axis_index("block")
        for slot in (1 - side, side):
            mine = pl.ds(pl.multiple_of(slot * share, share), share)
            shared = [ref[mine, :].astype(F32) for ref in grads]
            parts += [(at, shared) for at in range(first, taken)]
    tables = [own_table, far_table]
    for sub in range(2 * subs):
        low = 0
        for at, values in parts:
            height = values[0].shape[0]
            left_ref[low : low + height, sub * rows : (sub + 1) * rows] = pulled_of(
                values, tables[sub // subs], subs, blocks, sub % subs, at
            )
            low += height
    chunk = width // owners
    step = max(1, 256 // chunk) if cut else owners
    for rel in range(0, owners, step):
        columns = []
        for ref in (x_ref, y_ref):
            for sub in range(subs):
                pieces = [
                    ref[:, pl.ds(pl.multiple_of(sub * width + (lax.axis_index("sector") ^ at) * chunk, chunk), chunk)]
                    for at in range(rel, rel + step)
                ]
                columns.append(
                    jnp.concatenate(pieces, axis=1) if cut else ref[:, sub * width : (sub + 1) * width]
                )
        product = jnp.dot(
            left_ref[...], jnp.concatenate(columns, axis=0), preferred_element_type=F32
        )
        if not cut:
            outs[0][...] = product
            return
        straight, middle = first * chi, first * chi + crossing.shape[1]
        for at in range(step):
            lanes = slice(at * chunk, (at + 1) * chunk)
            out = outs[rel + at]
            partial = keep_ref[rel + at] + got_ref[rel + at].astype(F32)
            out[:straight] = product[:straight, lanes].astype(out.dtype)
            out[straight:] = partial.astype(BF16).astype(out.dtype)
            crossing[rel + at] = product[straight:middle, lanes].astype(crossing.dtype)
            staying[rel + at] = product[middle:, lanes].astype(staying.dtype)


def block_at(blocks, at):
    return lax.rem(lax.axis_index("rep") * (blocks // 2) + at, blocks)


def pulled_of(grads, table_ref, subs, blocks, sub, block):
    value = None
    for owner, grad in enumerate(grads):
        index = (owner * subs + sub) * blocks + block
        term = grad * count_of(table_ref, index, *grad.shape)
        value = term if value is None else value + term
    return value.astype(BF16)


def straight_kernel(*refs):
    out_ref, rest_ref = refs[-2:]
    value = total(*[ref[...] for ref in refs[:-3]])
    straight = out_ref.shape[0]
    out_ref[...] = value[:straight].astype(out_ref.dtype)
    rest_ref[...] = value[straight:].astype(rest_ref.dtype)


def shared_kernel(*refs):
    refs[-1][...] = total(*[ref[...] for ref in refs[:-1]]).astype(refs[-1].dtype)


def share_kernel(parts, upper_ref, over_ref, lower_ref, under_ref, unread, out_ref):
    side = lax.axis_index("block")
    straight = upper_ref.shape[0]
    out_ref[:straight] = total(upper_ref[...], over_ref[...]).astype(out_ref.dtype)
    share = lower_ref.shape[0] // parts
    for part in range(parts):
        for ref, slot in ((lower_ref, side), (under_ref, 1 - side)):
            low = pl.multiple_of(straight + (2 * part + slot) * share, share)
            out_ref[pl.ds(low, share)] = ref[part * share : (part + 1) * share]


def corner_kernel(owners, subs, blocks, site_ref, table_ref, *refs):
    grads = [ref[...].astype(F32).T for ref in refs[:owners]]
    out = refs[-1]
    rows = grads[0].shape[0]
    width = site_ref.shape[1]
    wide = jnp.concatenate([site_ref[block_at(blocks, block)] for block in range(blocks)], axis=1)
    left = jnp.concatenate(
        [
            jnp.concatenate(
                [pulled_of(grads, table_ref, subs, blocks, sub, block) for block in range(blocks)],
                axis=1,
            )
            for sub in range(subs)
        ],
        axis=0,
    )
    value = lax.dot_general(left, wide, NT, preferred_element_type=F32)
    for sub in range(subs):
        out[:, sub * width : (sub + 1) * width] = value[sub * rows : (sub + 1) * rows].astype(out.dtype)


def store_kernel(value_ref, unread, out_hbm, token_ref, stored):
    copy = pltpu.make_async_copy(value_ref, out_hbm, stored)
    copy.start()
    token_ref[...] = jnp.zeros(token_ref.shape, token_ref.dtype)
    copy.wait()


def per_device(corner, site, projector, cotangent, sector_dim, pair_dest, pair_sub, pair_site):
    owners = lax.axis_size("sector")
    sides = lax.axis_size("block")
    me, side, rep = lax.axis_index("sector"), lax.axis_index("block"), lax.axis_index("rep")
    blocks, width, chi = site.shape
    rows = corner.shape[1]
    subs = corner.shape[2] // width
    pairs = pair_dest.shape[0]
    direct = owners * chi == width and sides == 2 and blocks >= 8
    flat = corner[0]
    mine = blocks // 2
    first = mine // 2
    part = rows // 2
    chunk = width // owners
    places = owners * subs * blocks
    shape = jax.ShapeDtypeStruct
    other = swap(flat, "rep", 1)
    def table_of(value):
        if direct:
            stride = subs * blocks
            value = (value // stride ^ me) * stride + value % stride
        value = value // blocks * blocks + (value + rep * mine) % blocks
        hits = (jnp.arange(places, dtype=jnp.int32)[:, None] == value[None, :]).astype(BF16)
        return jnp.dot(hits, jnp.ones((pairs, 128), BF16), preferred_element_type=F32)

    sizes = (owners, subs, blocks)
    combo = (pair_dest * subs + pair_sub) * blocks + pair_site
    lanes = call(lanes_kernel, [shape((8, chi), jnp.int32)], [], flops=1 << 34)[0]
    grad, live = call(
        grad_kernel,
        [shape((chi, rows), BF16), shape((8, chi), F32)],
        [sector_dim, lanes, projector[0], cotangent[0]],
    )
    far = swap(combo, "rep", 1)
    if direct:
        grads = [grad] + [swap(grad, "sector", bit) for bit in range(1, owners)]
    else:
        shared = lax.all_gather(grad, "sector", axis=0)
        grads = [shared[owner] for owner in range(owners)]

    near, distant = table_of(combo), table_of(far)
    keep, send = call(
        functools.partial(forward_kernel, *sizes),
        [shape((owners, part, chi), F32), shape((owners, part, chi), BF16)],
        [near, flat, site],
        [
            pltpu.VMEM((2, 2 * part * subs, 2 * chi), F32),
            pltpu.VMEM((owners, part, chi), F32),
        ],
        flops=4 * subs * rows * width * chi * blocks,
    )
    got = swap(send, "rep", 1)

    def project(enlarged):
        value = jnp.dot(enlarged.astype(BF16), projector[0], preferred_element_type=F32)
        return (value * live[:1]).astype(BF16)

    def corner_term(after):
        return call(
            functools.partial(corner_kernel, *sizes),
            [shape((rows, subs * width), BF16)],
            [site, near, *grads],
            flops=2 * subs * rows * width * chi * owners,
            after=[after],
        )[0]

    if direct:
        share = (mine - first) * chi // sides
        height = first * chi + part
        outs = [shape((height, chunk), F32)] + [shape((height, chunk), BF16)] * (owners - 1)
        outs += [shape((owners, share, chunk), BF16), shape((owners, share, chunk), F32)]
    else:
        outs = [shape((mine * chi, width), F32)]
    pieces = call(
        functools.partial(site_kernel, *sizes, mine, first),
        outs,
        [near, distant, flat, other, keep, got, *grads],
        [pltpu.VMEM((mine * chi, 2 * subs * rows), BF16)],
        flops=4 * subs * rows * width * chi * mine,
    )
    if direct:
        bits = range(owners - 1, 0, -1)
        straight = first * chi
        crossed = swap(pieces[owners], "block", 1)
        direct_sums = [pieces[0]] + [swap(pieces[bit], "sector", bit) for bit in bits]
        merged = total(pieces[owners + 1], crossed)
        sent = merged.astype(BF16)
        shared_sums = [merged[0]] + [swap(sent[bit], "sector", bit) for bit in bits]
        corner_grad = corner_term(sent)
        upper, enlarged = call(
            straight_kernel,
            [shape((straight, chunk), BF16), shape((part, chunk), BF16)],
            direct_sums,
            after=[corner_grad],
        )
        over = swap(upper, "block", 1)
        projected = project(enlarged)
        lower = call(shared_kernel, [shape((share, chunk), BF16)], shared_sums)[0]
        under = swap(lower, "block", 1)
        corner_grad, token = call(
            store_kernel,
            [shape(corner_grad.shape, BF16), shape((8, chi), F32)],
            [corner_grad],
            [pltpu.SemaphoreType.DMA],
            after=[lower],
            stores=1,
        )
        own = call(
            functools.partial(share_kernel, mine - first),
            [shape((straight + share * sides, chunk), BF16)],
            [upper, over, lower, under],
            after=[token],
        )[0]
        projected = [projected, swap(projected, "rep", 1)]
        there = swap(own, "rep", 1)

        def ordered(pair):
            return jnp.where(rep == 0, jnp.stack(pair), jnp.stack(pair[::-1]))

        corner_new = ordered(projected).reshape(1, rows, chi)
        site_grad = ordered([own, there]).reshape(blocks, chi, chunk).swapaxes(1, 2).astype(F32)
    else:
        term = pieces[0].astype(BF16).reshape(mine, chi, width)
        term = lax.psum_scatter(term, "sector", scatter_dimension=2, tiled=True)
        term = lax.psum(term, "block")
        site_grad = lax.all_gather(term, "rep", axis=0, tiled=True).swapaxes(1, 2).astype(F32)
        partials = (keep + got.astype(F32)).astype(BF16)
        arrived = lax.all_to_all(partials, "sector", split_axis=0, concat_axis=0, tiled=True)
        projected = project(jnp.sum(arrived.astype(F32), axis=0))
        corner_new = lax.all_gather(projected, "rep", axis=0, tiled=True)[None]
        corner_grad = corner_term(term)
    return (corner_new, corner_grad[None], site_grad)


def solution(mesh):
    in_specs = (
        P(("groups", "sector"), "block", "rep"),
        P("groups", None, None),
        P(("groups", "sector"), None, None),
        P(("groups", "sector"), "block", None),
        P(("groups", "sector")),
        P(("groups", "sector", "rep")),
        P(("groups", "sector", "rep")),
        P(("groups", "sector", "rep")),
    )
    out_specs = (
        P(("groups", "sector"), "block", None),
        P(("groups", "sector"), "block", "rep"),
        P("groups", "sector", None),
    )
    return jax.shard_map(
        per_device, mesh=mesh, in_specs=in_specs, out_specs=out_specs, check_vma=False
    )
```

```python
import functools
import jax
import jax.numpy as jnp
from jax import lax
from jax.experimental import pallas as pl
from jax.experimental.pallas import tpu as pltpu
from jax.sharding import PartitionSpec as P

F32 = jnp.float32
BF16 = jnp.bfloat16
NT = (((1,), (1,)), ((), ()))
LIMIT = 28 * 1024 * 1024


def swap(value, axis, bit):
    size = lax.axis_size(axis)
    return lax.ppermute(value, axis, [(place, place ^ bit) for place in range(size)])


def total(*terms):
    acc = terms[0].astype(F32)
    for term in terms[1:]:
        acc = acc + term.astype(F32)
    return acc


def call(kernel, outs, args, scratch=(), flops=0, after=(), stores=0):
    args = [*args, *after]
    moved = sum(a.size * a.dtype.itemsize for a in args) + sum(
        a.size * a.dtype.itemsize for a in outs
    )
    scalars = pl.BlockSpec(memory_space=pltpu.SMEM)
    vectors = pl.BlockSpec(memory_space=pltpu.VMEM)
    return pl.pallas_call(
        kernel,
        out_shape=list(outs),
        in_specs=[scalars if a.ndim == 1 else vectors for a in args[: len(args) - len(after)]]
        + [pl.BlockSpec(memory_space=pl.ANY)] * len(after),
        out_specs=[pl.BlockSpec(memory_space=pltpu.HBM)] * stores + [vectors] * (len(outs) - stores),
        scratch_shapes=list(scratch),
        compiler_params=pltpu.CompilerParams(vmem_limit_bytes=LIMIT),
        cost_estimate=pl.CostEstimate(flops=flops if flops >> 34 else 0, bytes_accessed=moved, transcendentals=0),
    )(*args)


def count_of(table_ref, index, height, width):
    row = table_ref[pl.ds(index, 1), :]
    wide = jnp.concatenate([row] * (width // row.shape[1]), axis=1)
    return jnp.broadcast_to(wide, (height, width))


def lanes_kernel(out_ref):
    out_ref[...] = lax.broadcasted_iota(jnp.int32, out_ref.shape, 1)


def grad_kernel(dim_ref, lanes_ref, projector_ref, cotangent_ref, out_ref, live_ref):
    live = jnp.where(lanes_ref[...] < dim_ref[0], 1.0, 0.0)
    live_ref[...] = live
    masked = projector_ref[...].astype(F32) * live[:1]
    out_ref[...] = lax.dot_general(
        masked.astype(BF16), cotangent_ref[...], NT, preferred_element_type=F32
    ).astype(out_ref.dtype)


def forward_kernel(owners, subs, blocks, table_ref, x_ref, site_ref, keep_ref, send_ref, product_ref, sum_ref):
    rows, chi = keep_ref.shape[1:]
    width = site_ref.shape[1]
    step, tile = 2, 32
    rep = lax.axis_index("rep")
    stacked = jnp.concatenate(
        [
            x_ref[pl.ds(pl.multiple_of(half * rows, rows), rows), sub * width : (sub + 1) * width]
            for half in (1 - rep, rep)
            for sub in range(subs)
        ],
        axis=0,
    )
    for low in range(0, blocks, step):
        pair = jnp.concatenate(
            [site_ref[block_at(blocks, low + offset)] for offset in range(step)], axis=1
        )
        product_ref[low // step % 2] = jnp.dot(stacked, pair, preferred_element_type=F32)

        def add(at, low=low):
            for half, out_ref in ((1, keep_ref), (0, sum_ref)):
                pieces = [
                    product_ref[
                        low // step % 2,
                        pl.ds((half * subs + sub) * rows + at, tile),
                        offset * chi : (offset + 1) * chi,
                    ]
                    for sub in range(subs)
                    for offset in range(step)
                ]
                for owner in range(owners):
                    value = None
                    for sub in range(subs):
                        for offset in range(step):
                            index = (owner * subs + sub) * blocks + low + offset
                            term = pieces[sub * step + offset] * count_of(table_ref, index, tile, chi)
                            value = term if value is None else value + term
                    if low:
                        value = value + out_ref[owner, pl.ds(at, tile)]
                    out_ref[owner, pl.ds(at, tile)] = value

        if owners <= 4:
            for at in range(0, rows, tile):
                add(at)
        else:
            pl.loop(0, rows, step=tile)(lambda at: add(pl.multiple_of(at, tile)))
    send_ref[...] = sum_ref[...].astype(send_ref.dtype)


def site_kernel(
    owners, subs, blocks, taken, first, own_table, far_table, x_ref, y_ref, *refs
):
    grads, outs, left_ref = refs[:owners], refs[owners:-1], refs[-1]
    chi, rows = grads[0].shape
    width = x_ref.shape[1] // subs
    cut = len(outs) > 1
    whole = [ref[...].astype(F32) for ref in grads]
    parts = [(at, whole) for at in range(first if cut else taken)]
    if cut:
        crossing, staying = outs[owners:]
        share = crossing.shape[1] // (taken - first)
        side = lax.axis_index("block")
        for slot in (1 - side, side):
            mine = pl.ds(pl.multiple_of(slot * share, share), share)
            shared = [ref[mine, :].astype(F32) for ref in grads]
            parts += [(at, shared) for at in range(first, taken)]
    tables = [own_table, far_table]
    for sub in range(2 * subs):
        low = 0
        for at, values in parts:
            height = values[0].shape[0]
            left_ref[low : low + height, sub * rows : (sub + 1) * rows] = pulled_of(
                values, tables[sub // subs], subs, blocks, sub % subs, at
            )
            low += height
    chunk = width // owners
    step = max(1, 256 // chunk) if cut else owners
    for rel in range(0, owners, step):
        columns = []
        for ref in (x_ref, y_ref):
            for sub in range(subs):
                pieces = [
                    ref[:, pl.ds(pl.multiple_of(sub * width + (lax.axis_index("sector") ^ at) * chunk, chunk), chunk)]
                    for at in range(rel, rel + step)
                ]
                columns.append(
                    jnp.concatenate(pieces, axis=1) if cut else ref[:, sub * width : (sub + 1) * width]
                )
        product = jnp.dot(
            left_ref[...], jnp.concatenate(columns, axis=0), preferred_element_type=F32
        )
        if not cut:
            outs[0][...] = product
            return
        straight, middle = first * chi, first * chi + crossing.shape[1]
        for at in range(step):
            lanes = slice(at * chunk, (at + 1) * chunk)
            out = outs[rel + at]
            out[...] = product[:straight, lanes].astype(out.dtype)
            crossing[rel + at] = product[straight:middle, lanes].astype(crossing.dtype)
            staying[rel + at] = product[middle:, lanes].astype(staying.dtype)


def block_at(blocks, at):
    return lax.rem(lax.axis_index("rep") * (blocks // 2) + at, blocks)


def pulled_of(grads, table_ref, subs, blocks, sub, block):
    value = None
    for owner, grad in enumerate(grads):
        index = (owner * subs + sub) * blocks + block
        term = grad * count_of(table_ref, index, *grad.shape)
        value = term if value is None else value + term
    return value.astype(BF16)


def ride_kernel(keep_ref, got_ref, *refs):
    pieces, outs = refs[: len(refs) // 2], refs[len(refs) // 2 :]
    straight = pieces[0].shape[0]
    for at, (piece, out) in enumerate(zip(pieces, outs, strict=True)):
        out[:straight] = piece[...]
        out[straight:] = (keep_ref[at] + got_ref[at].astype(F32)).astype(BF16).astype(out.dtype)


def sum_kernel(count, *refs):
    out_ref, rest_ref = refs[-2:]
    upper, lower = [
        total(*[ref[...] for ref in part]) for part in (refs[:count], refs[count : 2 * count])
    ]
    straight = out_ref.shape[0] - lower.shape[0]
    out_ref[:straight] = upper[:straight].astype(out_ref.dtype)
    out_ref[straight:] = lower.astype(out_ref.dtype)
    rest_ref[...] = upper[straight:].astype(rest_ref.dtype)


def share_kernel(straight, parts, both_ref, beside_ref, unread, out_ref):
    side = lax.axis_index("block")
    out_ref[:straight] = total(both_ref[:straight], beside_ref[:straight]).astype(out_ref.dtype)
    share = (both_ref.shape[0] - straight) // parts
    for part in range(parts):
        for ref, slot in ((both_ref, side), (beside_ref, 1 - side)):
            low = pl.multiple_of(straight + (2 * part + slot) * share, share)
            out_ref[pl.ds(low, share)] = ref[straight + part * share : straight + (part + 1) * share]


def corner_kernel(owners, subs, blocks, site_ref, table_ref, *refs):
    grads = [ref[...].astype(F32).T for ref in refs[:owners]]
    out = refs[-1]
    rows = grads[0].shape[0]
    width = site_ref.shape[1]
    wide = jnp.concatenate([site_ref[block_at(blocks, block)] for block in range(blocks)], axis=1)
    left = jnp.concatenate(
        [
            jnp.concatenate(
                [pulled_of(grads, table_ref, subs, blocks, sub, block) for block in range(blocks)],
                axis=1,
            )
            for sub in range(subs)
        ],
        axis=0,
    )
    value = lax.dot_general(left, wide, NT, preferred_element_type=F32)
    for sub in range(subs):
        out[:, sub * width : (sub + 1) * width] = value[sub * rows : (sub + 1) * rows].astype(out.dtype)


def store_kernel(value_ref, unread, out_hbm, token_ref, stored):
    copy = pltpu.make_async_copy(value_ref, out_hbm, stored)
    copy.start()
    token_ref[...] = jnp.zeros(token_ref.shape, token_ref.dtype)
    copy.wait()


def per_device(corner, site, projector, cotangent, sector_dim, pair_dest, pair_sub, pair_site):
    owners = lax.axis_size("sector")
    sides = lax.axis_size("block")
    me, side, rep = lax.axis_index("sector"), lax.axis_index("block"), lax.axis_index("rep")
    blocks, width, chi = site.shape
    rows = corner.shape[1]
    subs = corner.shape[2] // width
    pairs = pair_dest.shape[0]
    direct = owners * chi == width and sides == 2 and blocks >= 8
    flat = corner[0]
    mine = blocks // 2
    first = mine // 4
    part = rows // 2
    chunk = width // owners
    places = owners * subs * blocks
    shape = jax.ShapeDtypeStruct
    other = swap(flat, "rep", 1)
    def table_of(value):
        if direct:
            stride = subs * blocks
            value = (value // stride ^ me) * stride + value % stride
        value = value // blocks * blocks + (value + rep * mine) % blocks
        hits = (jnp.arange(places, dtype=jnp.int32)[:, None] == value[None, :]).astype(BF16)
        return jnp.dot(hits, jnp.ones((pairs, 128), BF16), preferred_element_type=F32)

    sizes = (owners, subs, blocks)
    combo = (pair_dest * subs + pair_sub) * blocks + pair_site
    lanes = call(lanes_kernel, [shape((8, chi), jnp.int32)], [], flops=1 << 34)[0]
    grad, live = call(
        grad_kernel,
        [shape((chi, rows), BF16), shape((8, chi), F32)],
        [sector_dim, lanes, projector[0], cotangent[0]],
    )
    far = swap(combo, "rep", 1)
    if direct:
        grads = [grad] + [swap(grad, "sector", bit) for bit in range(1, owners)]
    else:
        shared = lax.all_gather(grad, "sector", axis=0)
        grads = [shared[owner] for owner in range(owners)]

    near, distant = table_of(combo), table_of(far)
    keep, send = call(
        functools.partial(forward_kernel, *sizes),
        [shape((owners, part, chi), F32), shape((owners, part, chi), BF16)],
        [near, flat, site],
        [
            pltpu.VMEM((2, 2 * part * subs, 2 * chi), F32),
            pltpu.VMEM((owners, part, chi), F32),
        ],
        flops=4 * subs * rows * width * chi * blocks,
    )
    got = swap(send, "rep", 1)

    def project(enlarged):
        value = jnp.dot(enlarged.astype(BF16), projector[0], preferred_element_type=F32)
        return (value * live[:1]).astype(BF16)

    def corner_term(after):
        return call(
            functools.partial(corner_kernel, *sizes),
            [shape((rows, subs * width), BF16)],
            [site, near, *grads],
            flops=2 * subs * rows * width * chi * owners,
            after=[after],
        )[0]

    if direct:
        share = (mine - first) * chi // sides
        straight = first * chi
        types = [F32] + [BF16] * (owners - 1)
        outs = [shape((straight, chunk), kind) for kind in types]
        outs += [shape((owners, share, chunk), BF16), shape((owners, share, chunk), F32)]
    else:
        outs = [shape((mine * chi, width), F32)]
    pieces = call(
        functools.partial(site_kernel, *sizes, mine, first),
        outs,
        [near, distant, flat, other, *grads],
        [pltpu.VMEM((mine * chi, 2 * subs * rows), BF16)],
        flops=4 * subs * rows * width * chi * mine,
    )
    if direct:
        bits = range(owners - 1, 0, -1)
        crossed = swap(pieces[owners], "block", 1)
        merged = total(pieces[owners + 1], crossed)
        pieces = call(
            ride_kernel,
            [shape((straight + part, chunk), kind) for kind in types],
            [keep, got, *pieces[:owners]],
        )
        direct_sums = [pieces[0]] + [swap(pieces[bit], "sector", bit) for bit in bits]
        sent = merged.astype(BF16)
        shared_sums = [merged[0]] + [swap(sent[bit], "sector", bit) for bit in (3, 1, 2)]
        corner_grad = corner_term(sent)
        both, enlarged = call(
            functools.partial(sum_kernel, owners),
            [shape((straight + share, chunk), BF16), shape((part, chunk), BF16)],
            [*direct_sums, *shared_sums],
            after=[corner_grad],
        )
        beside = swap(both, "block", 1)
        projected = project(enlarged)
        corner_grad, token = call(
            store_kernel,
            [shape(corner_grad.shape, BF16), shape((8, chi), F32)],
            [corner_grad],
            [pltpu.SemaphoreType.DMA],
            after=[both],
            stores=1,
        )
        own = call(
            functools.partial(share_kernel, straight, mine - first),
            [shape((straight + share * sides, chunk), BF16)],
            [both, beside],
            after=[token],
        )[0]
        projected = [projected, swap(projected, "rep", 1)]
        there = swap(own, "rep", 1)

        def ordered(pair):
            return jnp.where(rep == 0, jnp.stack(pair), jnp.stack(pair[::-1]))

        corner_new = ordered(projected).reshape(1, rows, chi)
        site_grad = ordered([own, there]).reshape(blocks, chi, chunk).swapaxes(1, 2).astype(F32)
    else:
        term = pieces[0].astype(BF16).reshape(mine, chi, width)
        term = lax.psum_scatter(term, "sector", scatter_dimension=2, tiled=True)
        term = lax.psum(term, "block")
        site_grad = lax.all_gather(term, "rep", axis=0, tiled=True).swapaxes(1, 2).astype(F32)
        partials = (keep + got.astype(F32)).astype(BF16)
        arrived = lax.all_to_all(partials, "sector", split_axis=0, concat_axis=0, tiled=True)
        projected = project(jnp.sum(arrived.astype(F32), axis=0))
        corner_new = lax.all_gather(projected, "rep", axis=0, tiled=True)[None]
        corner_grad = corner_term(term)
    return (corner_new, corner_grad[None], site_grad)


def solution(mesh):
    in_specs = (
        P(("groups", "sector"), "block", "rep"),
        P("groups", None, None),
        P(("groups", "sector"), None, None),
        P(("groups", "sector"), "block", None),
        P(("groups", "sector")),
        P(("groups", "sector", "rep")),
        P(("groups", "sector", "rep")),
        P(("groups", "sector", "rep")),
    )
    out_specs = (
        P(("groups", "sector"), "block", None),
        P(("groups", "sector"), "block", "rep"),
        P("groups", "sector", None),
    )
    return jax.shard_map(
        per_device, mesh=mesh, in_specs=in_specs, out_specs=out_specs, check_vma=False
    )
```
